512 devices in a mesh: aux: 16 (over z), orb: 32 (over y, x, core).
Axes of the slice: x: 4, y: 4, z: 16, core: 2. Of those that a mesh axis runs over, the one named last changes fastest.
Arguments:
- three_index: bfloat16 [2048, 896, 256], P(('aux', 'orb')), may hold values from -6 to 6
- tile_ids: int32 [512, 14, 4], P(('aux', 'orb')), may hold values from 0 to 14, as said below
- occupied: bfloat16 [896, 384], P('orb'), may hold values from -0.5 to 0.5
Outputs:
- exchange_matrix: float32 [896, 896], P('orb', 'aux')
The draws below stay inside these ranges and needn't reach their ends.
Inputs may be any that keep to these rules, and one draw needn't show every extreme that they name: `tile_ids`: each row tile's slots list distinct basis tiles first and then 14 in the empty slots; at least one slot is used; the first row tile of every slab uses all 4.
All inputs are finite; a program needn't handle non-finite values.
Results may differ from the reference program's by a relative error of at most 0.0003.
Values may be sent and summed in bfloat16 or wider, within the bound.
No kernel may reach another device: no remote copies, remote signals or barrier semaphores. Data moves between devices by JAX's collectives and lax.ppermute only.
A program may use at most 64 MiB of HBM per device.

```python
import jax
import jax.numpy as jnp
from jax import lax

TILE = 64
NB = 896
MT = 14
KEEP = 4
NOCC = 384
P_DEV = 4
NSLAB = 512
NAUX = 2048


def draw_tile_ids(key, part):
    key = jax.random.fold_in(key, 7)
    row_keys = jax.random.split(key, NSLAB * MT)
    orders = jax.vmap(lambda k: jax.random.permutation(k, MT)[:KEEP])(row_keys)
    counts = jax.random.randint(jax.random.fold_in(key, 1), (NSLAB * MT,), 1, KEEP + 1)
    rows = jnp.arange(NSLAB * MT, dtype=jnp.int32)
    counts = jnp.where(rows % MT == 0, KEEP, counts)
    slots = jnp.arange(KEEP, dtype=jnp.int32)[None, :]
    ids = jnp.where(slots < counts[:, None], orders, MT)
    return ids.reshape(NSLAB, MT, KEEP).astype(jnp.int32)


def shard_levels(rng, shape, cuts, smallest, largest):
    def one(axis_at, shards_of):
        steps = jax.random.uniform(jax.random.fold_in(jax.random.fold_in(rng, 6), axis_at), (shards_of,), jnp.float32, smallest / len(cuts), largest / len(cuts))
        return jnp.repeat(jnp.exp(steps), shape[axis_at] // shards_of).reshape((-1,) + (1,) * (len(shape) - axis_at - 1))

    gain = one(*cuts[0])
    for cut in cuts[1:]:
        gain = gain * one(*cut)
    return gain


def gaussian(stream_key, shape, deviation, limit, cuts=(), kind=jnp.bfloat16):
    factor_of = shard_levels(stream_key, shape, cuts, -0.22, 0.18) if cuts else 1.0
    result = jax.random.normal(stream_key, shape, jnp.float32) * deviation * factor_of
    return jnp.minimum(jnp.maximum(result, -limit), limit).astype(kind)


def setup_inputs(seed: int = 0) -> dict:
    seeds = jax.random.split(jax.random.key(seed), 4)
    return {
        "three_index": gaussian(seeds[0], (NAUX, NB, KEEP * TILE), 1.0, 6.0, ((0, 512),)),
        "tile_ids": draw_tile_ids(jax.random.fold_in(seeds[3], 71), 0),
        "occupied": gaussian(seeds[2], (NB, NOCC), 0.0625, 0.5, ((0, 32),)),
    }


def reference(three_index, tile_ids, occupied):
    padded = jnp.concatenate([occupied, jnp.zeros((TILE, NOCC), occupied.dtype)], axis=0)
    coef_tiles = padded.reshape(MT + 1, TILE, NOCC)
    slabs = three_index.reshape(NSLAB, P_DEV, MT, TILE, KEEP, TILE)

    def one_slab(total, item):
        block, ids = item
        chosen = coef_tiles[ids]
        half = jnp.einsum('pmrkl,mkli->mrpi', block.astype(jnp.float32), chosen.astype(jnp.float32), precision=lax.Precision.HIGHEST)
        half = half.reshape(NB, P_DEV * NOCC)
        return (total + jnp.dot(half, half.T, precision=lax.Precision.HIGHEST, preferred_element_type=jnp.float32), None)
    total, _ = lax.scan(one_slab, jnp.zeros((NB, NB), jnp.float32), (slabs, tile_ids))
    return total / jnp.sqrt(jnp.float32(NAUX * NOCC))
```

```python
import functools

import jax
import jax.numpy as jnp
from jax import lax
from jax.experimental import pallas as pl
from jax.experimental.pallas import tpu as pltpu
from jax.sharding import PartitionSpec as P

F32 = jnp.float32
BF16 = jnp.bfloat16
CODES = 128.0
TOP = 32767.0
TINY = 1e-30


def column_codes(block):
    largest = jnp.maximum(jnp.max(jnp.abs(block), axis=0, keepdims=True), TINY)
    return jnp.ceil(jnp.log2(largest) * CODES) + 1.0


def quantized(block, rows):
    row = lax.broadcasted_iota(jnp.int32, block.shape, 0)
    block = jnp.where(row < rows, block, 0.0)
    code = column_codes(block)
    scaled = jnp.round(block * (TOP * jnp.exp2(code * (-1.0 / CODES))))
    return jnp.where(row == rows, code, scaled)


def exchange_kernel(
    passes, ids_ref, core_ref, own_ref, sibling_ref, coef_ref, out_ref, half, high, low, mine_high, mine_low, total
):
    p_dev, basis, inner = own_ref.shape
    tiles, keep = ids_ref.shape[1] // 4, 4
    width = basis // tiles
    nocc = coef_ref.shape[1]
    groups, slot, _ = out_ref.shape
    rows = basis // groups // 2
    half[pl.ds(basis, half.shape[0] - basis), :] = jnp.zeros((half.shape[0] - basis, half.shape[1]), F32)
    for slab, ref in enumerate((own_ref, sibling_ref)):
        for t in range(tiles):
            picked = [
                coef_ref[pl.ds(pl.multiple_of(ids_ref[slab, t * keep + k] * width, width), width), :]
                for k in range(keep)
            ]
            chosen = jnp.concatenate(picked, axis=0)
            block = ref[:, pl.ds(t * width, width), :].reshape(p_dev * width, inner)
            product = jnp.dot(block, chosen, preferred_element_type=F32)
            for p in range(p_dev):
                piece = product[p * width : (p + 1) * width]
                where = (pl.ds(t * width, width), pl.ds(p * nocc, nocc))
                half[where] = piece
                top = piece.astype(BF16)
                high[where] = top
                if passes == 3:
                    low[where] = (piece - top.astype(F32)).astype(BF16)
        for core in range(2):

            @pl.when(core_ref[0] == core)
            def _():
                for g in range(groups):
                    piece = half[pl.ds((2 * g + core) * rows, slot), :]
                    top = piece.astype(BF16)
                    mine_high[pl.ds(g * slot, slot), :] = top
                    if passes == 3:
                        mine_low[pl.ds(g * slot, slot), :] = (piece - top.astype(F32)).astype(BF16)

        dims = (((1,), (1,)), ((), ()))
        for start in range(0, basis, 256):
            size = min(256, basis - start)
            cols = pl.ds(start, size)
            part = lax.dot_general(mine_high[...], high[cols, :], dims, preferred_element_type=F32)
            if passes == 3:
                part += lax.dot_general(mine_high[...], low[cols, :], dims, preferred_element_type=F32)
                part += lax.dot_general(mine_low[...], high[cols, :], dims, preferred_element_type=F32)
            if slab == 0:
                total[:, cols] = part
            else:
                total[:, cols] += part
    for g in range(groups):
        block = total[pl.ds(g * slot, slot), :]
        out_ref[g] = quantized(block, rows).astype(jnp.int32).astype(jnp.int16)


def group_sum_kernel(rows, columns, in_ref, out_ref):
    groups, slot, basis = in_ref.shape
    total = jnp.zeros((slot, basis), F32)
    for g in range(groups):
        block = in_ref[g].astype(jnp.int32).astype(F32)
        total += block * (jnp.exp2(block[rows : rows + 1] * (1.0 / CODES)) * (1.0 / TOP))
    coded = quantized(total, rows)
    coded = jnp.concatenate([coded, jnp.zeros((slot, 128), F32)], axis=1)
    lane = lax.broadcasted_iota(jnp.int32, (slot // 2, 128), 1)
    for j in range(out_ref.shape[0]):
        first = j * columns // 128 * 128
        shift = j * columns - first
        window = coded[:, first : first + 256]
        if shift:
            window = pltpu.roll(window, 256 - shift, 1)
        window = window[:, :128]
        lower = pltpu.roll(window[slot // 2 :], 64, 1)
        out_ref[j] = jnp.where(lane < 64, window[: slot // 2], lower).astype(jnp.int32).astype(jnp.int16)


def final_sum_kernel(scale, in_ref, out_ref):
    parts, half_slot, _ = in_ref.shape
    rows, columns = out_ref.shape
    lane = lax.broadcasted_iota(jnp.int32, (1, 128), 1)
    total = jnp.zeros((half_slot, 128), F32)
    for z in range(parts):
        block = in_ref[z].astype(jnp.int32).astype(F32)
        code = block[rows - half_slot : rows - half_slot + 1]
        code = jnp.where(lane < 64, pltpu.roll(code, 64, 1), code)
        total += block * jnp.exp2(code * (1.0 / CODES))
    total = total * (scale / TOP)
    out_ref[0:half_slot, :] = total[:, :columns]
    lower = pltpu.roll(total, 64, 1)
    out_ref[half_slot:rows, :] = lower[: rows - half_slot, :columns]


VMEM = pl.BlockSpec(memory_space=pltpu.VMEM)
SMEM = pl.BlockSpec(memory_space=pltpu.SMEM)


def per_device(passes, three_index, tile_ids, occupied):
    p_dev, basis, inner = three_index.shape
    tiles, keep = tile_ids.shape[1:]
    width = inner // keep
    rows, nocc = occupied.shape
    n_orb = lax.axis_size("orb")
    n_aux = lax.axis_size("aux")
    chips = n_orb // 2
    columns = basis // n_aux
    slot = 32
    me = lax.axis_index("orb")
    core, chip = me % 2, me // 2
    across = [[2 * g + c for g in range(chips)] for c in range(2)]
    pairs = [[2 * g, 2 * g + 1] for g in range(chips)]

    with jax.named_scope("sibling_slab"):
        sibling = lax.ppermute(three_index, "orb", [(i, i ^ 1) for i in range(n_orb)])
    with jax.named_scope("gather_coefficients"):
        ids = tile_ids.reshape(1, tiles * keep)
        tail = jnp.pad(ids.astype(BF16), ((0, slot - rows - 1), (0, nocc - tiles * keep)))
        mine = jnp.concatenate([occupied, tail], axis=0)
        spread = jnp.broadcast_to(mine[None], (chips, slot, nocc))
        same_core = lax.all_to_all(spread, "orb", 0, 0, axis_index_groups=across, tiled=True)
        both = lax.all_gather(same_core, "orb", axis=0, axis_index_groups=pairs)
        coef = both[:, :, :rows].transpose(1, 0, 2, 3).reshape(basis, nocc)
        coef = jnp.concatenate([coef, jnp.zeros((width, nocc), BF16)], axis=0)
        theirs = lax.dynamic_slice(both, (1 - core, chip, rows, 0), (1, 1, 1, tiles * keep))
        ids = jnp.concatenate([ids, theirs.reshape(1, tiles * keep).astype(jnp.int32)], axis=0)

    depth = p_dev * nocc
    with jax.named_scope("exchange"):
        coded = pl.pallas_call(
            functools.partial(exchange_kernel, passes),
            out_shape=jax.ShapeDtypeStruct((chips, slot, basis), jnp.int16),
            in_specs=[SMEM, SMEM, VMEM, VMEM, VMEM],
            out_specs=VMEM,
            scratch_shapes=[
                pltpu.VMEM((basis + 8, depth), F32),
                pltpu.VMEM((basis, depth), BF16),
                pltpu.VMEM((basis, depth), BF16),
                pltpu.VMEM((chips * slot, depth), BF16),
                pltpu.VMEM((chips * slot, depth), BF16),
                pltpu.VMEM((chips * slot, basis), F32),
            ],
            compiler_params=pltpu.CompilerParams(vmem_limit_bytes=48 * 1024 * 1024),
        )(ids, core.reshape(1).astype(jnp.int32), three_index, sibling, coef)
    with jax.named_scope("sum_over_chips"):
        coded = lax.all_to_all(coded, "orb", 0, 0, axis_index_groups=across, tiled=True)
        coded = pl.pallas_call(
            functools.partial(group_sum_kernel, rows, columns),
            out_shape=jax.ShapeDtypeStruct((n_aux, slot // 2, 128), jnp.int16),
            in_specs=[VMEM],
            out_specs=VMEM,
            compiler_params=pltpu.CompilerParams(vmem_limit_bytes=32 * 1024 * 1024),
        )(coded)
    with jax.named_scope("sum_over_aux"):
        coded = lax.all_to_all(coded, "aux", 0, 0, tiled=True)
        total_aux = p_dev * n_aux * n_orb
        return pl.pallas_call(
            functools.partial(final_sum_kernel, float(total_aux * nocc) ** -0.5),
            out_shape=jax.ShapeDtypeStruct((rows, columns), F32),
            in_specs=[VMEM],
            out_specs=VMEM,
        )(coded)


def solution(mesh):
    return jax.shard_map(
        functools.partial(per_device, 3),
        mesh=mesh,
        in_specs=(P(("aux", "orb"), None, None), P(("aux", "orb"), None, None), P("orb", None)),
        out_specs=P("orb", "aux"),
        check_vma=False,
    )
```

```python
import functools

import jax
import jax.numpy as jnp
from jax import lax
from jax.experimental import pallas as pl
from jax.experimental.pallas import tpu as pltpu
from jax.sharding import PartitionSpec as P

F32 = jnp.float32
BF16 = jnp.bfloat16
CODES = 128.0
TOP = 32767.0
TINY = 1e-30
FIRST_CHIP = 10
FIRST_AUX = 8


def column_codes(block):
    largest = jnp.maximum(jnp.max(jnp.abs(block), axis=0, keepdims=True), TINY)
    return jnp.ceil(jnp.log2(largest) * CODES) + 1.0


def quantized(block, rows):
    row = lax.broadcasted_iota(jnp.int32, block.shape, 0)
    block = jnp.where(row < rows, block, 0.0)
    code = column_codes(block)
    scaled = jnp.round(block * (TOP * jnp.exp2(code * (-1.0 / CODES))))
    return jnp.where(row == rows, code, scaled)


def spread_kernel(ids_ref, occupied_ref, out_ref, block):
    groups = out_ref.shape[0]
    rows, nocc = occupied_ref.shape
    keep, tiles = ids_ref.shape
    block[...] = jnp.zeros(block.shape, F32)
    block[pl.ds(0, rows), :] = occupied_ref[...].astype(F32)
    block[pl.ds(rows, keep), pl.ds(0, tiles)] = ids_ref[...].astype(F32)
    value = block[...].astype(BF16)
    for g in range(groups):
        out_ref[g] = value


def exchange_kernel(first, ids_ref, core_ref, own_ref, sibling_ref, both_ref, out_ref, sibling, coef, half, mine, arrived):
    p_dev, basis, inner = own_ref.shape
    groups = out_ref.shape[0]
    keep, tiles = ids_ref.shape[0] // 2, ids_ref.shape[1]
    width = basis // tiles
    nocc = both_ref.shape[3]
    rows = basis // groups // 2
    copy = pltpu.make_async_copy(sibling_ref, sibling, arrived)
    copy.start()
    for g in range(groups):
        for core in range(2):
            chip = (g + first) % groups
            coef[pl.ds((2 * chip + core) * rows, rows), :] = both_ref[core, g, pl.ds(0, rows), :]
    coef[pl.ds(basis, width), :] = jnp.zeros((width, nocc), BF16)
    for slab, ref in enumerate((own_ref, sibling)):
        if slab == 1:
            copy.wait()
        for t in range(tiles):
            picked = [
                coef[pl.ds(pl.multiple_of(ids_ref[slab * keep + k, t] * width, width), width), :] for k in range(keep)
            ]
            block = ref[:, pl.ds(t * width, width), :].reshape(p_dev * width, inner)
            product = jnp.dot(block, jnp.concatenate(picked, axis=0), preferred_element_type=F32).astype(BF16)
            for p in range(p_dev):
                where = (pl.ds(t * width, width), pl.ds((slab * p_dev + p) * nocc, nocc))
                half[where] = product[p * width : (p + 1) * width]
    for core in range(2):

        @pl.when(core_ref[0] == core)
        def _():
            for g in range(groups):
                chip = (g + first) % groups
                mine[pl.ds(g * rows, rows), :] = half[pl.ds((2 * chip + core) * rows, rows), :]

    for start in range(0, basis, 256):
        size = min(256, basis - start)
        part = lax.dot_general(
            mine[...], half[pl.ds(start, size), :], (((1,), (1,)), ((), ())), preferred_element_type=F32
        )
        for g in range(groups):
            block = part[g * rows : (g + 1) * rows]
            block = jnp.concatenate([block, jnp.zeros((out_ref.shape[1] - rows, size), F32)], axis=0)
            out_ref[g, :, pl.ds(start, size)] = quantized(block, rows).astype(jnp.int32).astype(jnp.int16)


def group_sum_kernel(first, rows, columns, in_ref, out_ref):
    groups, slot, basis = in_ref.shape
    total = jnp.zeros((slot, basis), F32)
    for g in range(groups):
        block = in_ref[g].astype(jnp.int32).astype(F32)
        total += block * (jnp.exp2(block[rows : rows + 1] * (1.0 / CODES)) * (1.0 / TOP))
    coded = quantized(total, rows)
    coded = jnp.concatenate([coded, jnp.zeros((slot, 128), F32)], axis=1)
    lane = lax.broadcasted_iota(jnp.int32, (slot // 2, 128), 1)
    for j in range(out_ref.shape[0]):
        start = (j + first) % out_ref.shape[0] * columns
        base = start // 128 * 128
        shift = start - base
        window = coded[:, base : base + 256]
        if shift:
            window = pltpu.roll(window, 256 - shift, 1)
        window = window[:, :128]
        lower = pltpu.roll(window[slot // 2 :], 64, 1)
        out_ref[j] = jnp.where(lane < 64, window[: slot // 2], lower).astype(jnp.int32).astype(jnp.int16)


def final_sum_kernel(scale, in_ref, out_ref):
    parts, half_slot, _ = in_ref.shape
    rows, columns = out_ref.shape
    lane = lax.broadcasted_iota(jnp.int32, (1, 128), 1)
    total = jnp.zeros((half_slot, 128), F32)
    for z in range(parts):
        block = in_ref[z].astype(jnp.int32).astype(F32)
        code = block[rows - half_slot : rows - half_slot + 1]
        code = jnp.where(lane < 64, pltpu.roll(code, 64, 1), code)
        total += block * jnp.exp2(code * (1.0 / CODES))
    total = total * (scale / TOP)
    out_ref[0:half_slot, :] = total[:, :columns]
    lower = pltpu.roll(total, 64, 1)
    out_ref[half_slot:rows, :] = lower[: rows - half_slot, :columns]


VMEM = pl.BlockSpec(memory_space=pltpu.VMEM)
SMEM = pl.BlockSpec(memory_space=pltpu.SMEM)


def per_device(three_index, tile_ids, occupied):
    p_dev, basis, inner = three_index.shape
    tiles, keep = tile_ids.shape[1:]
    width = inner // keep
    rows, nocc = occupied.shape
    n_orb = lax.axis_size("orb")
    n_aux = lax.axis_size("aux")
    chips = n_orb // 2
    columns = basis // n_aux
    slot = 32
    me = lax.axis_index("orb")
    core, chip = me % 2, me // 2
    across = [[2 * ((g + FIRST_CHIP) % chips) + c for g in range(chips)] for c in range(2)]
    along = [[(z + FIRST_AUX) % n_aux for z in range(n_aux)]]
    pairs = [[2 * g, 2 * g + 1] for g in range(chips)]

    with jax.named_scope("spread_coefficients"):
        ids = tile_ids[0].T
        spread = pl.pallas_call(
            spread_kernel,
            out_shape=jax.ShapeDtypeStruct((chips, slot, nocc), BF16),
            in_specs=[VMEM, VMEM],
            out_specs=VMEM,
            scratch_shapes=[pltpu.VMEM((slot, nocc), F32)],
            compiler_params=pltpu.CompilerParams(vmem_limit_bytes=4 * 1024 * 1024),
        )(ids, occupied)
    with jax.named_scope("sibling_slab"):
        spread, slab = lax.optimization_barrier((spread, three_index))
        sibling = lax.ppermute(slab, "orb", [(i, i ^ 1) for i in range(n_orb)])
    with jax.named_scope("gather_coefficients"):
        same_core = lax.all_to_all(spread, "orb", 0, 0, axis_index_groups=across, tiled=True)
        both = lax.all_gather(same_core, "orb", axis=0, axis_index_groups=pairs)
        theirs = lax.dynamic_slice(both, (1 - core, (chip + chips - FIRST_CHIP) % chips, rows, 0), (1, 1, keep, tiles))
        ids = jnp.concatenate([ids, theirs.reshape(keep, tiles).astype(jnp.int32)], axis=0)

    depth = 2 * p_dev * nocc
    with jax.named_scope("exchange"):
        coded = pl.pallas_call(
            functools.partial(exchange_kernel, FIRST_CHIP),
            out_shape=jax.ShapeDtypeStruct((chips, slot, basis), jnp.int16),
            in_specs=[SMEM, SMEM, VMEM, pl.BlockSpec(memory_space=pl.ANY), VMEM],
            out_specs=VMEM,
            scratch_shapes=[
                pltpu.VMEM(three_index.shape, BF16),
                pltpu.VMEM((basis + width, nocc), BF16),
                pltpu.VMEM((basis, depth), BF16),
                pltpu.VMEM((chips * rows, depth), BF16),
                pltpu.SemaphoreType.DMA,
            ],
            compiler_params=pltpu.CompilerParams(vmem_limit_bytes=32 * 1024 * 1024),
        )(ids, core.reshape(1).astype(jnp.int32), three_index, sibling, both)
    with jax.named_scope("sum_over_chips"):
        coded = lax.all_to_all(coded, "orb", 0, 0, axis_index_groups=across, tiled=True)
        coded = pl.pallas_call(
            functools.partial(group_sum_kernel, FIRST_AUX, rows, columns),
            out_shape=jax.ShapeDtypeStruct((n_aux, slot // 2, 128), jnp.int16),
            in_specs=[VMEM],
            out_specs=VMEM,
            compiler_params=pltpu.CompilerParams(vmem_limit_bytes=8 * 1024 * 1024),
        )(coded)
    with jax.named_scope("sum_over_aux"):
        coded = lax.all_to_all(coded, "aux", 0, 0, axis_index_groups=along, tiled=True)
        total_aux = p_dev * n_aux * n_orb
        return pl.pallas_call(
            functools.partial(final_sum_kernel, float(total_aux * nocc) ** -0.5),
            out_shape=jax.ShapeDtypeStruct((rows, columns), F32),
            in_specs=[VMEM],
            out_specs=VMEM,
            compiler_params=pltpu.CompilerParams(vmem_limit_bytes=4 * 1024 * 1024),
        )(coded)


def solution(mesh):
    return jax.shard_map(
        per_device,
        mesh=mesh,
        in_specs=(P(("aux", "orb"), None, None), P(("aux", "orb"), None, None), P("orb", None)),
        out_specs=P("orb", "aux"),
        check_vma=False,
    )
```

```python
import functools

import jax
import jax.numpy as jnp
from jax import lax
from jax.experimental import pallas as pl
from jax.experimental.pallas import tpu as pltpu
from jax.sharding import PartitionSpec as P

F32 = jnp.float32
BF16 = jnp.bfloat16
CODES = 128.0
TOP = 32767.0
TINY = 1e-30
FIRST_CHIP = 10
FIRST_AUX = 8


def wire_rows(rows, basis):
    chunks = basis // 128
    return rows * chunks + (chunks + 1) // 2


def stacked(block):
    return jnp.concatenate([block[:, c : c + 128] for c in range(0, block.shape[1], 128)], axis=0)


def coded(block):
    largest = jnp.maximum(jnp.max(jnp.abs(block), axis=0, keepdims=True), TINY)
    code = jnp.ceil(jnp.log2(largest) * CODES) + 1.0
    return jnp.round(block * (TOP * jnp.exp2(code * (-1.0 / CODES)))), code


def scale_of(code):
    return jnp.exp2(code * (1.0 / CODES)) * (1.0 / TOP)


def as_int16(block):
    return block.astype(jnp.int32).astype(jnp.int16)


def as_float(block):
    return block.astype(jnp.int32).astype(F32)


def pieces(rows, basis):
    for start in range(0, basis, 256):
        yield start, start // 128 * rows, rows * min(2, (basis - start) // 128)


def write_piece(out_ref, g, codes, place, first, block, last):
    values, code = coded(block)
    if not last:
        codes[g, pl.ds(place, 1), :] = code
        out_ref[g, pl.ds(first, block.shape[0]), :] = as_int16(values)
    else:
        values = jnp.concatenate([values, codes[g, pl.ds(0, place), :], code], axis=0)
        out_ref[g, pl.ds(first, values.shape[0]), :] = as_int16(values)


def spread_kernel(occupied_ref, out_ref):
    block = occupied_ref[...].astype(F32)
    rest = jnp.zeros((out_ref.shape[1] - block.shape[0], block.shape[1]), F32)
    block = jnp.concatenate([block, rest], axis=0).astype(BF16)
    for g in range(out_ref.shape[0]):
        out_ref[g] = block


def rows_of_core(first, groups, half, core_ref, other, mine):
    rows = mine.shape[0] // groups
    for core in range(2):

        @pl.when(core_ref[0] == core)
        def _():
            for g in range(groups):
                chip = (g + first) % groups
                mine[pl.ds(g * rows, rows), :] = half[pl.ds((2 * chip + (core ^ other)) * rows, rows), :]


def product_chunks(mine, half):
    basis = half.shape[0]
    for start in range(0, basis, 256):
        cols = pl.ds(start, min(256, basis - start))
        yield lax.dot_general(mine[...], half[cols, :], (((1,), (1,)), ((), ())), preferred_element_type=F32)


def half_kernel(first, ids_ref, core_ref, own_ref, both_ref, half_ref, out_ref, coef, mine, codes):
    p_dev, basis, inner = own_ref.shape
    groups = out_ref.shape[0]
    keep, tiles = ids_ref.shape
    width = basis // tiles
    nocc = both_ref.shape[3]
    rows = basis // groups // 2
    for g in range(groups):
        chip = (g + first) % groups
        for core in range(2):
            coef[pl.ds((2 * chip + core) * rows, rows), :] = both_ref[core, g, pl.ds(0, rows), :]
    coef[pl.ds(basis, width), :] = jnp.zeros((width, nocc), BF16)
    for t in range(tiles):
        picked = [coef[pl.ds(pl.multiple_of(ids_ref[k, t] * width, width), width), :] for k in range(keep)]
        block = own_ref[:, pl.ds(t * width, width), :].reshape(p_dev * width, inner)
        product = jnp.dot(block, jnp.concatenate(picked, axis=0), preferred_element_type=F32).astype(BF16)
        for p in range(p_dev):
            half_ref[pl.ds(t * width, width), pl.ds(p * nocc, nocc)] = product[p * width : (p + 1) * width]
    rows_of_core(first, groups, half_ref, core_ref, 1, mine)
    for place, (part, (start, row, _)) in enumerate(zip(product_chunks(mine, half_ref), pieces(rows, basis))):
        for g in range(groups):
            block = stacked(part[g * rows : (g + 1) * rows])
            write_piece(out_ref, g, codes, place, row, block, start + 256 >= basis)


def own_rows_kernel(first, core_ref, half_ref, out_ref, mine):
    groups = out_ref.shape[0]
    basis = half_ref.shape[0]
    rows = basis // groups // 2
    rows_of_core(first, groups, half_ref, core_ref, 0, mine)
    for part, (_, row, size) in zip(product_chunks(mine, half_ref), pieces(rows, basis)):
        for g in range(groups):
            out_ref[g, pl.ds(row, size), :] = stacked(part[g * rows : (g + 1) * rows])


def pair_sum_kernel(rows, basis, part_ref, in_ref, out_ref, codes):
    groups, length, _ = out_ref.shape
    for g in range(groups):
        theirs = as_float(in_ref[g])
        for place, (start, row, size) in enumerate(pieces(rows, basis)):
            code = theirs[rows * (basis // 128) + place :][:1]
            block = part_ref[g, pl.ds(row, size), :] + theirs[row : row + size] * scale_of(code)
            write_piece(out_ref, g, codes, place, row, block, start + 256 >= basis)


def group_sum_kernel(first, rows, columns, in_ref, out_ref):
    groups, length, _ = in_ref.shape
    parts, half_slot, _ = out_ref.shape
    basis = parts * columns
    totals = [0.0 for _ in pieces(rows, basis)]
    for g in range(groups):
        theirs = as_float(in_ref[g])
        for place, (start, row, size) in enumerate(pieces(rows, basis)):
            code = theirs[rows * (basis // 128) + place :][:1]
            totals[place] += theirs[row : row + size] * scale_of(code)
    chunks = [t[c : c + rows] for t in totals for c in range(0, t.shape[0], rows)]
    values, code = coded(jnp.concatenate(chunks, axis=1))
    rest = jnp.broadcast_to(code, (2 * half_slot - rows, basis))
    both = jnp.concatenate([values, rest], axis=0)
    both = jnp.concatenate([both, jnp.zeros((2 * half_slot, 128), F32)], axis=1)
    lane = lax.broadcasted_iota(jnp.int32, (half_slot, 128), 1)
    for j in range(parts):
        start = (j + first) % parts * columns
        base = start // 128 * 128
        shift = start - base
        window = both[:, base : base + 256]
        if shift:
            window = pltpu.roll(window, 256 - shift, 1)
        window = window[:, :128]
        lower = pltpu.roll(window[half_slot:], 64, 1)
        out_ref[j] = as_int16(jnp.where(lane < 64, window[:half_slot], lower))


def final_sum_kernel(scale, in_ref, out_ref):
    parts, half_slot, _ = in_ref.shape
    rows, columns = out_ref.shape
    lane = lax.broadcasted_iota(jnp.int32, (1, 128), 1)
    total = jnp.zeros((half_slot, 128), F32)
    for z in range(parts):
        block = as_float(in_ref[z])
        code = block[rows - half_slot : rows - half_slot + 1]
        code = jnp.where(lane < 64, pltpu.roll(code, 64, 1), code)
        total += block * jnp.exp2(code * (1.0 / CODES))
    total = total * (scale / TOP)
    out_ref[0:half_slot, :] = total[:, :columns]
    lower = pltpu.roll(total, 64, 1)
    out_ref[half_slot:rows, :] = lower[: rows - half_slot, :columns]


VMEM = pl.BlockSpec(memory_space=pltpu.VMEM)
SMEM = pl.BlockSpec(memory_space=pltpu.SMEM)


def per_device(three_index, tile_ids, occupied):
    p_dev, basis, inner = three_index.shape
    tiles, keep = tile_ids.shape[1:]
    width = inner // keep
    rows, nocc = occupied.shape
    n_orb = lax.axis_size("orb")
    n_aux = lax.axis_size("aux")
    chips = n_orb // 2
    columns = basis // n_aux
    slot = 32
    me = lax.axis_index("orb")
    core = me % 2
    across = [[2 * ((g + FIRST_CHIP) % chips) + c for g in range(chips)] for c in range(2)]
    along = [[(z + FIRST_AUX) % n_aux for z in range(n_aux)]]
    pairs = [[2 * g, 2 * g + 1] for g in range(chips)]

    with jax.named_scope("gather_coefficients"):
        spread = pl.pallas_call(
            spread_kernel,
            out_shape=jax.ShapeDtypeStruct((chips, slot, nocc), BF16),
            in_specs=[VMEM],
            out_specs=VMEM,
            compiler_params=pltpu.CompilerParams(vmem_limit_bytes=4 * 1024 * 1024),
        )(occupied)
        same_core = lax.all_to_all(spread, "orb", 0, 0, axis_index_groups=across, tiled=True)
        both = lax.all_gather(same_core, "orb", axis=0, axis_index_groups=pairs)

    depth = p_dev * nocc
    core = core.reshape(1).astype(jnp.int32)
    wire = (chips, wire_rows(rows, basis), 128)
    sent = jax.ShapeDtypeStruct(wire, jnp.int16)
    codes = pltpu.VMEM((chips, 8, 128), F32)
    flops = basis * basis * depth
    with jax.named_scope("half"):
        half, theirs = pl.pallas_call(
            functools.partial(half_kernel, FIRST_CHIP),
            out_shape=(jax.ShapeDtypeStruct((basis, depth), BF16), sent),
            in_specs=[SMEM, SMEM, VMEM, VMEM],
            out_specs=(VMEM, VMEM),
            scratch_shapes=[pltpu.VMEM((basis + width, nocc), BF16), pltpu.VMEM((chips * rows, depth), BF16), codes],
            compiler_params=pltpu.CompilerParams(vmem_limit_bytes=24 * 1024 * 1024),
            cost_estimate=pl.CostEstimate(flops=2 * flops, bytes_accessed=0, transcendentals=0),
        )(tile_ids[0].T, core, three_index, both)
    with jax.named_scope("sibling_rows"):
        theirs = lax.ppermute(theirs, "orb", [(i, i ^ 1) for i in range(n_orb)])
    with jax.named_scope("own_rows"):
        part = pl.pallas_call(
            functools.partial(own_rows_kernel, FIRST_CHIP),
            out_shape=jax.ShapeDtypeStruct(wire, F32),
            in_specs=[SMEM, VMEM],
            out_specs=VMEM,
            scratch_shapes=[pltpu.VMEM((chips * rows, depth), BF16)],
            compiler_params=pltpu.CompilerParams(vmem_limit_bytes=16 * 1024 * 1024),
            cost_estimate=pl.CostEstimate(flops=flops, bytes_accessed=0, transcendentals=0),
        )(core, half)
    with jax.named_scope("pair_sum"):
        sums = pl.pallas_call(
            functools.partial(pair_sum_kernel, rows, basis),
            out_shape=sent,
            in_specs=[VMEM, VMEM],
            out_specs=VMEM,
            scratch_shapes=[codes],
            compiler_params=pltpu.CompilerParams(vmem_limit_bytes=8 * 1024 * 1024),
        )(part, theirs)
    with jax.named_scope("sum_over_chips"):
        sums = lax.all_to_all(sums, "orb", 0, 0, axis_index_groups=across, tiled=True)
        sums = pl.pallas_call(
            functools.partial(group_sum_kernel, FIRST_AUX, rows, columns),
            out_shape=jax.ShapeDtypeStruct((n_aux, slot // 2, 128), jnp.int16),
            in_specs=[VMEM],
            out_specs=VMEM,
            compiler_params=pltpu.CompilerParams(vmem_limit_bytes=8 * 1024 * 1024),
        )(sums)
    with jax.named_scope("sum_over_aux"):
        sums = lax.all_to_all(sums, "aux", 0, 0, axis_index_groups=along, tiled=True)
        total_aux = p_dev * n_aux * n_orb
        return pl.pallas_call(
            functools.partial(final_sum_kernel, float(total_aux * nocc) ** -0.5),
            out_shape=jax.ShapeDtypeStruct((rows, columns), F32),
            in_specs=[VMEM],
            out_specs=VMEM,
            compiler_params=pltpu.CompilerParams(vmem_limit_bytes=4 * 1024 * 1024),
        )(sums)


def solution(mesh):
    return jax.shard_map(
        per_device,
        mesh=mesh,
        in_specs=(P(("aux", "orb"), None, None), P(("aux", "orb"), None, None), P("orb", None)),
        out_specs=P("orb", "aux"),
        check_vma=False,
    )
```

```python
import functools

import jax
import jax.numpy as jnp
from jax import lax
from jax.experimental import pallas as pl
from jax.experimental.pallas import tpu as pltpu
from jax.sharding import PartitionSpec as P

F32 = jnp.float32
BF16 = jnp.bfloat16
CODES = 128.0
TOP = 32767.0
TINY = 1e-30
FIRST_CHIP = 10
FIRST_AUX = 8
ORDER_COST = 20_000_000_000


def wire_rows(rows, basis):
    chunks = basis // 128
    return rows * chunks + (chunks + 1) // 2


def stacked(block):
    return jnp.concatenate([block[:, c : c + 128] for c in range(0, block.shape[1], 128)], axis=0)


def coded(block):
    largest = jnp.maximum(jnp.max(jnp.abs(block), axis=0, keepdims=True), TINY)
    code = jnp.ceil(jnp.log2(largest) * CODES) + 1.0
    return jnp.round(block * (TOP * jnp.exp2(code * (-1.0 / CODES)))), code


def scale_of(code):
    return jnp.exp2(code * (1.0 / CODES)) * (1.0 / TOP)


def as_int16(block):
    return block.astype(jnp.int32).astype(jnp.int16)


def as_float(block):
    return block.astype(jnp.int32).astype(F32)


def pieces(rows, basis):
    for start in range(0, basis, 256):
        yield start, start // 128 * rows, rows * min(2, (basis - start) // 128)


def write_piece(out_ref, g, codes, place, first, block, last):
    values, code = coded(block)
    if not last:
        codes[g, pl.ds(place, 1), :] = code
        out_ref[g, pl.ds(first, block.shape[0]), :] = as_int16(values)
    else:
        values = jnp.concatenate([values, codes[g, pl.ds(0, place), :], code], axis=0)
        out_ref[g, pl.ds(first, values.shape[0]), :] = as_int16(values)


def spread_kernel(ids_ref, occupied_ref, out_ref):
    keep, tiles = ids_ref.shape
    chunks = stacked(occupied_ref[...].astype(F32))
    tail = jnp.concatenate([ids_ref[...].astype(F32), jnp.zeros((keep, 128 - tiles), F32)], axis=1)
    rest = jnp.zeros((out_ref.shape[1] - chunks.shape[0] - keep, 128), F32)
    block = jnp.concatenate([chunks, tail] + [rest] * (rest.shape[0] > 0), axis=0).astype(BF16)
    for g in range(out_ref.shape[0]):
        out_ref[g] = block


def own_rows(first, groups, half, core_ref, mine):
    rows = mine.shape[0] // groups
    for core in range(2):

        @pl.when(core_ref[0] == core)
        def _():
            for g in range(groups):
                chip = (g + first) % groups
                mine[pl.ds(g * rows, rows), :] = half[pl.ds((2 * chip + core) * rows, rows), :]


def product_chunks(mine, half):
    basis = half.shape[0]
    for start in range(0, basis, 256):
        cols = pl.ds(start, min(256, basis - start))
        yield cols, lax.dot_general(mine[...], half[cols, :], (((1,), (1,)), ((), ())), preferred_element_type=F32)


def half_transform(ids_ref, slab_ref, coef, half, first_column):
    p_dev, basis, inner = slab_ref.shape
    keep, tiles = ids_ref.shape
    width = basis // tiles
    nocc = coef.shape[1]
    for t in range(tiles):
        picked = [coef[pl.ds(pl.multiple_of(ids_ref[k, t] * width, width), width), :] for k in range(keep)]
        block = slab_ref[:, pl.ds(t * width, width), :].reshape(p_dev * width, inner)
        product = jnp.dot(block, jnp.concatenate(picked, axis=0), preferred_element_type=F32).astype(BF16)
        for p in range(p_dev):
            half[pl.ds(t * width, width), pl.ds(first_column + p * nocc, nocc)] = product[p * width : (p + 1) * width]


def hold_kernel(slab_ref, out_ref):
    for p in range(slab_ref.shape[0]):
        out_ref[p] = slab_ref[p]


def order_kernel(first, basis, both_ref, coef):
    groups = both_ref.shape[1]
    rows = basis // groups // 2
    for g in range(groups):
        chip = (g + first) % groups
        for core in range(2):
            for c in range(coef.shape[1] // 128):
                place = (pl.ds((2 * chip + core) * rows, rows), pl.ds(c * 128, 128))
                coef[place] = both_ref[core, g, pl.ds(c * rows, rows), :]
    rest = coef.shape[0] - basis
    coef[pl.ds(basis, rest), :] = jnp.zeros((rest, coef.shape[1]), BF16)


def exchange_kernel(first, ids_ref, their_ids_ref, core_ref, coef, own_ref, sibling_ref, out_ref, half, mine, codes):
    groups = out_ref.shape[0]
    basis = half.shape[0]
    rows = basis // groups // 2
    half_transform(ids_ref, own_ref, coef, half, 0)
    half_transform(their_ids_ref, sibling_ref, coef, half, half.shape[1] // 2)
    own_rows(first, groups, half, core_ref, mine)
    for place, ((cols, part), (start, row, _)) in enumerate(zip(product_chunks(mine, half), pieces(rows, basis))):
        for g in range(groups):
            block = stacked(part[g * rows : (g + 1) * rows])
            write_piece(out_ref, g, codes, place, row, block, start + 256 >= basis)


def group_sum_kernel(first, rows, columns, in_ref, out_ref):
    groups, length, _ = in_ref.shape
    parts, half_slot, _ = out_ref.shape
    basis = parts * columns
    totals = [0.0 for _ in pieces(rows, basis)]
    for g in range(groups):
        theirs = as_float(in_ref[g])
        for place, (start, row, size) in enumerate(pieces(rows, basis)):
            code = theirs[rows * (basis // 128) + place :][:1]
            totals[place] += theirs[row : row + size] * scale_of(code)
    chunks = [t[c : c + rows] for t in totals for c in range(0, t.shape[0], rows)]
    values, code = coded(jnp.concatenate(chunks, axis=1))
    rest = jnp.broadcast_to(code, (2 * half_slot - rows, basis))
    both = jnp.concatenate([values, rest], axis=0)
    both = jnp.concatenate([both, jnp.zeros((2 * half_slot, 128), F32)], axis=1)
    lane = lax.broadcasted_iota(jnp.int32, (half_slot, 128), 1)
    for j in range(parts):
        start = (j + first) % parts * columns
        base = start // 128 * 128
        shift = start - base
        window = both[:, base : base + 256]
        if shift:
            window = pltpu.roll(window, 256 - shift, 1)
        window = window[:, :128]
        lower = pltpu.roll(window[half_slot:], 64, 1)
        out_ref[j] = as_int16(jnp.where(lane < 64, window[:half_slot], lower))


def final_sum_kernel(scale, in_ref, out_ref):
    parts, half_slot, _ = in_ref.shape
    rows, columns = out_ref.shape
    lane = lax.broadcasted_iota(jnp.int32, (1, 128), 1)
    total = jnp.zeros((half_slot, 128), F32)
    for z in range(parts):
        block = as_float(in_ref[z])
        code = block[rows - half_slot : rows - half_slot + 1]
        code = jnp.where(lane < 64, pltpu.roll(code, 64, 1), code)
        total += block * jnp.exp2(code * (1.0 / CODES))
    total = total * (scale / TOP)
    out_ref[0:half_slot, :] = total[:, :columns]
    lower = pltpu.roll(total, 64, 1)
    out_ref[half_slot:rows, :] = lower[: rows - half_slot, :columns]


VMEM = pl.BlockSpec(memory_space=pltpu.VMEM)
SMEM = pl.BlockSpec(memory_space=pltpu.SMEM)


def per_device(three_index, tile_ids, occupied):
    p_dev, basis, inner = three_index.shape
    tiles, keep = tile_ids.shape[1:]
    width = inner // keep
    rows, nocc = occupied.shape
    n_orb = lax.axis_size("orb")
    n_aux = lax.axis_size("aux")
    chips = n_orb // 2
    columns = basis // n_aux
    slot = 32
    me = lax.axis_index("orb")
    core, chip = me % 2, me // 2
    across = [[2 * ((g + FIRST_CHIP) % chips) + c for g in range(chips)] for c in range(2)]
    along = [[(z + FIRST_AUX) % n_aux for z in range(n_aux)]]
    pairs = [[2 * g, 2 * g + 1] for g in range(chips)]

    with jax.named_scope("gather_coefficients"):
        length = rows * nocc // 128 + keep
        length += -length % 8
        ids = tile_ids[0].T
        spread = pl.pallas_call(
            spread_kernel,
            out_shape=jax.ShapeDtypeStruct((chips, length, 128), BF16),
            in_specs=[VMEM, VMEM],
            out_specs=VMEM,
        )(ids, occupied)
        spread, slab = lax.optimization_barrier((spread, three_index))
        own = pl.pallas_call(
            hold_kernel,
            out_shape=jax.ShapeDtypeStruct(slab.shape, BF16),
            in_specs=[VMEM],
            out_specs=VMEM,
            compiler_params=pltpu.CompilerParams(vmem_limit_bytes=8 * 1024 * 1024),
        )(slab)
        own, slab = lax.optimization_barrier((own, slab))
        same_core = lax.all_to_all(spread, "orb", 0, 0, axis_index_groups=across, tiled=True)
        both = lax.all_gather(same_core, "orb", axis=0, axis_index_groups=pairs)
        place = (chip + chips - FIRST_CHIP) % chips
        pair = [
            lax.dynamic_slice(both, (c, place, rows * nocc // 128, 0), (1, 1, keep, tiles))
            for c in (core, 1 - core)
        ]
        ids, theirs = (i.reshape(keep, tiles).astype(jnp.int32) for i in pair)
    with jax.named_scope("sibling_slab"):
        sibling = lax.ppermute(slab, "orb", [(i, i ^ 1) for i in range(n_orb)])

    depth = 2 * p_dev * nocc
    core = core.reshape(1).astype(jnp.int32)
    wire = (chips, wire_rows(rows, basis), 128)
    with jax.named_scope("order_coefficients"):
        coef = pl.pallas_call(
            functools.partial(order_kernel, FIRST_CHIP, basis),
            out_shape=jax.ShapeDtypeStruct((basis + width, nocc), BF16),
            in_specs=[VMEM],
            out_specs=VMEM,
            compiler_params=pltpu.CompilerParams(vmem_limit_bytes=8 * 1024 * 1024),
            cost_estimate=pl.CostEstimate(flops=ORDER_COST, bytes_accessed=0, transcendentals=0),
        )(both)
    with jax.named_scope("exchange"):
        sums = pl.pallas_call(
            functools.partial(exchange_kernel, FIRST_CHIP),
            out_shape=jax.ShapeDtypeStruct(wire, jnp.int16),
            in_specs=[SMEM, SMEM, SMEM, VMEM, VMEM, VMEM],
            out_specs=VMEM,
            scratch_shapes=[
                pltpu.VMEM((basis, depth), BF16),
                pltpu.VMEM((chips * rows, depth), BF16),
                pltpu.VMEM((chips, 8, 128), F32),
            ],
            compiler_params=pltpu.CompilerParams(vmem_limit_bytes=12 * 1024 * 1024),
        )(ids, theirs, core, coef, own, sibling)
    with jax.named_scope("sum_over_chips"):
        sums = lax.all_to_all(sums, "orb", 0, 0, axis_index_groups=across, tiled=True)
        sums = pl.pallas_call(
            functools.partial(group_sum_kernel, FIRST_AUX, rows, columns),
            out_shape=jax.ShapeDtypeStruct((n_aux, slot // 2, 128), jnp.int16),
            in_specs=[VMEM],
            out_specs=VMEM,
            compiler_params=pltpu.CompilerParams(vmem_limit_bytes=8 * 1024 * 1024),
        )(sums)
    with jax.named_scope("sum_over_aux"):
        sums = lax.all_to_all(sums, "aux", 0, 0, axis_index_groups=along, tiled=True)
        total_aux = p_dev * n_aux * n_orb
        return pl.pallas_call(
            functools.partial(final_sum_kernel, float(total_aux * nocc) ** -0.5),
            out_shape=jax.ShapeDtypeStruct((rows, columns), F32),
            in_specs=[VMEM],
            out_specs=VMEM,
            compiler_params=pltpu.CompilerParams(vmem_limit_bytes=4 * 1024 * 1024),
        )(sums)


def solution(mesh):
    return jax.shard_map(
        per_device,
        mesh=mesh,
        in_specs=(P(("aux", "orb"), None, None), P(("aux", "orb"), None, None), P("orb", None)),
        out_specs=P("orb", "aux"),
        check_vma=False,
    )
```

```python
import functools

import jax
import jax.numpy as jnp
from jax import lax
from jax.experimental import pallas as pl
from jax.experimental.pallas import tpu as pltpu
from jax.sharding import PartitionSpec as P

F32 = jnp.float32
BF16 = jnp.bfloat16
CODES = 128.0
TOP = 32767.0
TINY = 1e-30
FIRST_CHIP = 10
FIRST_AUX = 9
ORDER_COST = 20_000_000_000


def wire_rows(rows, basis):
    chunks = basis // 128
    return rows * chunks + (chunks + 1) // 2


def stacked(block):
    return jnp.concatenate([block[:, c : c + 128] for c in range(0, block.shape[1], 128)], axis=0)


def coded(block):
    largest = jnp.maximum(jnp.max(jnp.abs(block), axis=0, keepdims=True), TINY)
    code = jnp.ceil(jnp.log2(largest) * CODES) + 1.0
    return jnp.round(block * (TOP * jnp.exp2(code * (-1.0 / CODES)))), code


def scale_of(code):
    return jnp.exp2(code * (1.0 / CODES)) * (1.0 / TOP)


def as_int16(block):
    return block.astype(jnp.int32).astype(jnp.int16)


def as_float(block):
    return block.astype(jnp.int32).astype(F32)


def pieces(rows, basis):
    for start in range(0, basis, 256):
        yield start, start // 128 * rows, rows * min(2, (basis - start) // 128)


def write_piece(out_ref, g, codes, place, first, block, last):
    values, code = coded(block)
    if not last:
        codes[g, pl.ds(place, 1), :] = code
        out_ref[g, pl.ds(first, block.shape[0]), :] = as_int16(values)
    else:
        values = jnp.concatenate([values, codes[g, pl.ds(0, place), :], code], axis=0)
        out_ref[g, pl.ds(first, values.shape[0]), :] = as_int16(values)


def spread_kernel(ids_ref, occupied_ref, out_ref):
    keep, tiles = ids_ref.shape
    chunks = stacked(occupied_ref[...].astype(F32))
    tail = jnp.concatenate([ids_ref[...].astype(F32), jnp.zeros((keep, 128 - tiles), F32)], axis=1)
    rest = jnp.zeros((out_ref.shape[1] - chunks.shape[0] - keep, 128), F32)
    block = jnp.concatenate([chunks, tail] + [rest] * (rest.shape[0] > 0), axis=0).astype(BF16)
    for g in range(out_ref.shape[0]):
        out_ref[g] = block


def own_rows(first, groups, half, core_ref, mine):
    rows = mine.shape[0] // groups
    for core in range(2):

        @pl.when(core_ref[0] == core)
        def _():
            for g in range(groups):
                chip = (g + first) % groups
                mine[pl.ds(g * rows, rows), :] = half[pl.ds((2 * chip + core) * rows, rows), :]


def product_chunks(mine, half):
    basis = half.shape[0]
    for start in range(0, basis, 256):
        cols = pl.ds(start, min(256, basis - start))
        yield cols, lax.dot_general(mine[...], half[cols, :], (((1,), (1,)), ((), ())), preferred_element_type=F32)


def half_transform(ids_ref, slab_ref, coef, half, first_column):
    p_dev, basis, inner = slab_ref.shape
    keep, tiles = ids_ref.shape
    width = basis // tiles
    nocc = coef.shape[1]
    for t in range(tiles):
        picked = [coef[pl.ds(pl.multiple_of(ids_ref[k, t] * width, width), width), :] for k in range(keep)]
        block = slab_ref[:, pl.ds(t * width, width), :].reshape(p_dev * width, inner)
        product = jnp.dot(block, jnp.concatenate(picked, axis=0), preferred_element_type=F32).astype(BF16)
        for p in range(p_dev):
            half[pl.ds(t * width, width), pl.ds(first_column + p * nocc, nocc)] = product[p * width : (p + 1) * width]


def hold_kernel(slab_ref, out_ref):
    for p in range(slab_ref.shape[0]):
        out_ref[p] = slab_ref[p]


def order_kernel(first, basis, both_ref, coef):
    groups = both_ref.shape[1]
    rows = basis // groups // 2
    for g in range(groups):
        chip = (g + first) % groups
        for core in range(2):
            for c in range(coef.shape[1] // 128):
                place = (pl.ds((2 * chip + core) * rows, rows), pl.ds(c * 128, 128))
                coef[place] = both_ref[core, g, pl.ds(c * rows, rows), :]
    rest = coef.shape[0] - basis
    coef[pl.ds(basis, rest), :] = jnp.zeros((rest, coef.shape[1]), BF16)


def exchange_kernel(first, ids_ref, their_ids_ref, core_ref, coef, own_ref, sibling_ref, out_ref, half, mine, codes):
    groups = out_ref.shape[0]
    basis = half.shape[0]
    rows = basis // groups // 2
    half_transform(ids_ref, own_ref, coef, half, 0)
    half_transform(their_ids_ref, sibling_ref, coef, half, half.shape[1] // 2)
    own_rows(first, groups, half, core_ref, mine)
    for place, ((cols, part), (start, row, _)) in enumerate(zip(product_chunks(mine, half), pieces(rows, basis))):
        for g in range(groups):
            block = stacked(part[g * rows : (g + 1) * rows])
            write_piece(out_ref, g, codes, place, row, block, start + 256 >= basis)


def group_sum_kernel(first, rows, columns, in_ref, out_ref):
    groups, length, _ = in_ref.shape
    parts, half_slot, _ = out_ref.shape
    basis = parts * columns
    totals = [0.0 for _ in pieces(rows, basis)]
    for g in range(groups):
        theirs = as_float(in_ref[g])
        for place, (start, row, size) in enumerate(pieces(rows, basis)):
            code = theirs[rows * (basis // 128) + place :][:1]
            totals[place] += theirs[row : row + size] * scale_of(code)
    chunks = [t[c : c + rows] for t in totals for c in range(0, t.shape[0], rows)]
    values, code = coded(jnp.concatenate(chunks, axis=1))
    rest = jnp.broadcast_to(code, (2 * half_slot - rows, basis))
    both = jnp.concatenate([values, rest], axis=0)
    both = jnp.concatenate([both, jnp.zeros((2 * half_slot, 128), F32)], axis=1)
    lane = lax.broadcasted_iota(jnp.int32, (half_slot, 128), 1)
    for j in range(parts):
        start = (j + first) % parts * columns
        base = start // 128 * 128
        shift = start - base
        window = both[:, base : base + 256]
        if shift:
            window = pltpu.roll(window, 256 - shift, 1)
        window = window[:, :128]
        lower = pltpu.roll(window[half_slot:], 64, 1)
        out_ref[j] = as_int16(jnp.where(lane < 64, window[:half_slot], lower))


def final_sum_kernel(scale, in_ref, out_ref):
    parts, half_slot, _ = in_ref.shape
    rows, columns = out_ref.shape
    lane = lax.broadcasted_iota(jnp.int32, (1, 128), 1)
    total = jnp.zeros((half_slot, 128), F32)
    for z in range(parts):
        block = as_float(in_ref[z])
        code = block[rows - half_slot : rows - half_slot + 1]
        code = jnp.where(lane < 64, pltpu.roll(code, 64, 1), code)
        total += block * jnp.exp2(code * (1.0 / CODES))
    total = total * (scale / TOP)
    out_ref[0:half_slot, :] = total[:, :columns]
    lower = pltpu.roll(total, 64, 1)
    out_ref[half_slot:rows, :] = lower[: rows - half_slot, :columns]


VMEM = pl.BlockSpec(memory_space=pltpu.VMEM)
SMEM = pl.BlockSpec(memory_space=pltpu.SMEM)


def per_device(three_index, tile_ids, occupied):
    p_dev, basis, inner = three_index.shape
    tiles, keep = tile_ids.shape[1:]
    width = inner // keep
    rows, nocc = occupied.shape
    n_orb = lax.axis_size("orb")
    n_aux = lax.axis_size("aux")
    chips = n_orb // 2
    columns = basis // n_aux
    slot = 32
    me = lax.axis_index("orb")
    core, chip = me % 2, me // 2
    across = [[2 * ((g + FIRST_CHIP) % chips) + c for g in range(chips)] for c in range(2)]
    along = [[(z + FIRST_AUX) % n_aux for z in range(n_aux)]]
    pairs = [[2 * g, 2 * g + 1] for g in range(chips)]

    with jax.named_scope("gather_coefficients"):
        length = rows * nocc // 128 + keep
        length += -length % 8
        ids = tile_ids[0].T
        spread = pl.pallas_call(
            spread_kernel,
            out_shape=jax.ShapeDtypeStruct((chips, length, 128), BF16),
            in_specs=[VMEM, VMEM],
            out_specs=VMEM,
        )(ids, occupied)
        spread, slab = lax.optimization_barrier((spread, three_index))
        own = pl.pallas_call(
            hold_kernel,
            out_shape=jax.ShapeDtypeStruct(slab.shape, BF16),
            in_specs=[VMEM],
            out_specs=VMEM,
            compiler_params=pltpu.CompilerParams(vmem_limit_bytes=8 * 1024 * 1024),
        )(slab)
        own, slab = lax.optimization_barrier((own, slab))
        same_core = lax.all_to_all(spread, "orb", 0, 0, axis_index_groups=across, tiled=True)
        both = lax.all_gather(same_core, "orb", axis=0, axis_index_groups=pairs)
        place = (chip + chips - FIRST_CHIP) % chips
        pair = [
            lax.dynamic_slice(both, (c, place, rows * nocc // 128, 0), (1, 1, keep, tiles))
            for c in (core, 1 - core)
        ]
        ids, theirs = (i.reshape(keep, tiles).astype(jnp.int32) for i in pair)
    with jax.named_scope("sibling_slab"):
        sibling = lax.ppermute(slab, "orb", [(i, i ^ 1) for i in range(n_orb)])

    depth = 2 * p_dev * nocc
    core = core.reshape(1).astype(jnp.int32)
    wire = (chips, wire_rows(rows, basis), 128)
    with jax.named_scope("order_coefficients"):
        coef = pl.pallas_call(
            functools.partial(order_kernel, FIRST_CHIP, basis),
            out_shape=jax.ShapeDtypeStruct((basis + width, nocc), BF16),
            in_specs=[VMEM],
            out_specs=VMEM,
            compiler_params=pltpu.CompilerParams(vmem_limit_bytes=8 * 1024 * 1024),
            cost_estimate=pl.CostEstimate(flops=ORDER_COST, bytes_accessed=0, transcendentals=0),
        )(both)
    with jax.named_scope("exchange"):
        sums = pl.pallas_call(
            functools.partial(exchange_kernel, FIRST_CHIP),
            out_shape=jax.ShapeDtypeStruct(wire, jnp.int16),
            in_specs=[SMEM, SMEM, SMEM, VMEM, VMEM, VMEM],
            out_specs=VMEM,
            scratch_shapes=[
                pltpu.VMEM((basis, depth), BF16),
                pltpu.VMEM((chips * rows, depth), BF16),
                pltpu.VMEM((chips, 8, 128), F32),
            ],
            compiler_params=pltpu.CompilerParams(vmem_limit_bytes=12 * 1024 * 1024),
        )(ids, theirs, core, coef, own, sibling)
    with jax.named_scope("sum_over_chips"):
        sums = lax.all_to_all(sums, "orb", 0, 0, axis_index_groups=across, tiled=True)
        sums = pl.pallas_call(
            functools.partial(group_sum_kernel, FIRST_AUX, rows, columns),
            out_shape=jax.ShapeDtypeStruct((n_aux, slot // 2, 128), jnp.int16),
            in_specs=[VMEM],
            out_specs=VMEM,
            compiler_params=pltpu.CompilerParams(vmem_limit_bytes=8 * 1024 * 1024),
        )(sums)
    with jax.named_scope("sum_over_aux"):
        sums = lax.all_to_all(sums, "aux", 0, 0, axis_index_groups=along, tiled=True)
        total_aux = p_dev * n_aux * n_orb
        return pl.pallas_call(
            functools.partial(final_sum_kernel, float(total_aux * nocc) ** -0.5),
            out_shape=jax.ShapeDtypeStruct((rows, columns), F32),
            in_specs=[VMEM],
            out_specs=VMEM,
            compiler_params=pltpu.CompilerParams(vmem_limit_bytes=4 * 1024 * 1024),
        )(sums)


def solution(mesh):
    return jax.shard_map(
        per_device,
        mesh=mesh,
        in_specs=(P(("aux", "orb"), None, None), P(("aux", "orb"), None, None), P("orb", None)),
        out_specs=P("orb", "aux"),
        check_vma=False,
    )
```

```python
import functools

import jax
import jax.numpy as jnp
from jax import lax
from jax.experimental import pallas as pl
from jax.experimental.pallas import tpu as pltpu
from jax.sharding import PartitionSpec as P

F32 = jnp.float32
BF16 = jnp.bfloat16
CODES = 128.0
TOP = 32767.0
TINY = 1e-30
FIRST_CHIP = (14, 10)
FIRST_AUX = 9
ORDER_COST = 20_000_000_000


def wire_rows(rows, basis):
    chunks = basis // 128
    return rows * chunks + (chunks + 1) // 2


def stacked(block):
    return jnp.concatenate([block[:, c : c + 128] for c in range(0, block.shape[1], 128)], axis=0)


def coded(block):
    largest = jnp.maximum(jnp.max(jnp.abs(block), axis=0, keepdims=True), TINY)
    code = jnp.ceil(jnp.log2(largest) * CODES) + 1.0
    return jnp.round(block * (TOP * jnp.exp2(code * (-1.0 / CODES)))), code


def scale_of(code):
    return jnp.exp2(code * (1.0 / CODES)) * (1.0 / TOP)


def as_int16(block):
    return block.astype(jnp.int32).astype(jnp.int16)


def as_float(block):
    return block.astype(jnp.int32).astype(F32)


def pieces(rows, basis):
    for start in range(0, basis, 256):
        yield start, start // 128 * rows, rows * min(2, (basis - start) // 128)


def write_piece(out_ref, g, codes, place, first, block, last):
    values, code = coded(block)
    if not last:
        codes[g, pl.ds(place, 1), :] = code
        out_ref[g, pl.ds(first, block.shape[0]), :] = as_int16(values)
    else:
        values = jnp.concatenate([values, codes[g, pl.ds(0, place), :], code], axis=0)
        out_ref[g, pl.ds(first, values.shape[0]), :] = as_int16(values)


def spread_kernel(ids_ref, occupied_ref, out_ref):
    keep, tiles = ids_ref.shape
    chunks = stacked(occupied_ref[...].astype(F32))
    tail = jnp.concatenate([ids_ref[...].astype(F32), jnp.zeros((keep, 128 - tiles), F32)], axis=1)
    rest = jnp.zeros((out_ref.shape[1] - chunks.shape[0] - keep, 128), F32)
    block = jnp.concatenate([chunks, tail] + [rest] * (rest.shape[0] > 0), axis=0).astype(BF16)
    for g in range(out_ref.shape[0]):
        out_ref[g] = block


def own_rows(first, groups, half, core_ref, mine):
    rows = mine.shape[0] // groups
    for core in range(2):

        @pl.when(core_ref[0] == core)
        def _():
            for g in range(groups):
                chip = (g + first[core]) % groups
                mine[pl.ds(g * rows, rows), :] = half[pl.ds((2 * chip + core) * rows, rows), :]


def product_chunks(mine, half):
    basis = half.shape[0]
    for start in range(0, basis, 256):
        cols = pl.ds(start, min(256, basis - start))
        yield cols, lax.dot_general(mine[...], half[cols, :], (((1,), (1,)), ((), ())), preferred_element_type=F32)


def half_transform(ids_ref, slab_ref, coef, half, first_column):
    p_dev, basis, inner = slab_ref.shape
    keep, tiles = ids_ref.shape
    width = basis // tiles
    nocc = coef.shape[1]
    for t in range(tiles):
        picked = [coef[pl.ds(pl.multiple_of(ids_ref[k, t] * width, width), width), :] for k in range(keep)]
        block = slab_ref[:, pl.ds(t * width, width), :].reshape(p_dev * width, inner)
        product = jnp.dot(block, jnp.concatenate(picked, axis=0), preferred_element_type=F32).astype(BF16)
        for p in range(p_dev):
            half[pl.ds(t * width, width), pl.ds(first_column + p * nocc, nocc)] = product[p * width : (p + 1) * width]


def hold_kernel(slab_ref, out_ref):
    for p in range(slab_ref.shape[0]):
        out_ref[p] = slab_ref[p]


def order_kernel(first, basis, both_ref, coef):
    groups = both_ref.shape[1]
    rows = basis // groups // 2
    for g in range(groups):
        for core in range(2):
            chip = (g + first[core]) % groups
            for c in range(coef.shape[1] // 128):
                place = (pl.ds((2 * chip + core) * rows, rows), pl.ds(c * 128, 128))
                coef[place] = both_ref[core, g, pl.ds(c * rows, rows), :]
    rest = coef.shape[0] - basis
    coef[pl.ds(basis, rest), :] = jnp.zeros((rest, coef.shape[1]), BF16)


def exchange_kernel(first, ids_ref, their_ids_ref, core_ref, coef, own_ref, sibling_ref, out_ref, half, mine, codes):
    groups = out_ref.shape[0]
    basis = half.shape[0]
    rows = basis // groups // 2
    half_transform(ids_ref, own_ref, coef, half, 0)
    half_transform(their_ids_ref, sibling_ref, coef, half, half.shape[1] // 2)
    own_rows(first, groups, half, core_ref, mine)
    for place, ((cols, part), (start, row, _)) in enumerate(zip(product_chunks(mine, half), pieces(rows, basis))):
        for g in range(groups):
            block = stacked(part[g * rows : (g + 1) * rows])
            write_piece(out_ref, g, codes, place, row, block, start + 256 >= basis)


def group_sum_kernel(first, rows, columns, in_ref, out_ref):
    groups, length, _ = in_ref.shape
    parts, half_slot, _ = out_ref.shape
    basis = parts * columns
    totals = [0.0 for _ in pieces(rows, basis)]
    for g in range(groups):
        theirs = as_float(in_ref[g])
        for place, (start, row, size) in enumerate(pieces(rows, basis)):
            code = theirs[rows * (basis // 128) + place :][:1]
            totals[place] += theirs[row : row + size] * scale_of(code)
    chunks = [t[c : c + rows] for t in totals for c in range(0, t.shape[0], rows)]
    values, code = coded(jnp.concatenate(chunks, axis=1))
    rest = jnp.broadcast_to(code, (2 * half_slot - rows, basis))
    both = jnp.concatenate([values, rest], axis=0)
    both = jnp.concatenate([both, jnp.zeros((2 * half_slot, 128), F32)], axis=1)
    lane = lax.broadcasted_iota(jnp.int32, (half_slot, 128), 1)
    for j in range(parts):
        start = (j + first) % parts * columns
        base = start // 128 * 128
        shift = start - base
        window = both[:, base : base + 256]
        if shift:
            window = pltpu.roll(window, 256 - shift, 1)
        window = window[:, :128]
        lower = pltpu.roll(window[half_slot:], 64, 1)
        out_ref[j] = as_int16(jnp.where(lane < 64, window[:half_slot], lower))


def final_sum_kernel(scale, in_ref, out_ref):
    parts, half_slot, _ = in_ref.shape
    rows, columns = out_ref.shape
    lane = lax.broadcasted_iota(jnp.int32, (1, 128), 1)
    total = jnp.zeros((half_slot, 128), F32)
    for z in range(parts):
        block = as_float(in_ref[z])
        code = block[rows - half_slot : rows - half_slot + 1]
        code = jnp.where(lane < 64, pltpu.roll(code, 64, 1), code)
        total += block * jnp.exp2(code * (1.0 / CODES))
    total = total * (scale / TOP)
    out_ref[0:half_slot, :] = total[:, :columns]
    lower = pltpu.roll(total, 64, 1)
    out_ref[half_slot:rows, :] = lower[: rows - half_slot, :columns]


VMEM = pl.BlockSpec(memory_space=pltpu.VMEM)
SMEM = pl.BlockSpec(memory_space=pltpu.SMEM)


def per_device(three_index, tile_ids, occupied):
    p_dev, basis, inner = three_index.shape
    tiles, keep = tile_ids.shape[1:]
    width = inner // keep
    rows, nocc = occupied.shape
    n_orb = lax.axis_size("orb")
    n_aux = lax.axis_size("aux")
    chips = n_orb // 2
    columns = basis // n_aux
    slot = 32
    me = lax.axis_index("orb")
    core, chip = me % 2, me // 2
    across = [[2 * ((g + FIRST_CHIP[c]) % chips) + c for g in range(chips)] for c in range(2)]
    along = [[(z + FIRST_AUX) % n_aux for z in range(n_aux)]]
    pairs = [[2 * g, 2 * g + 1] for g in range(chips)]

    with jax.named_scope("gather_coefficients"):
        length = rows * nocc // 128 + keep
        length += -length % 8
        ids = tile_ids[0].T
        spread = pl.pallas_call(
            spread_kernel,
            out_shape=jax.ShapeDtypeStruct((chips, length, 128), BF16),
            in_specs=[VMEM, VMEM],
            out_specs=VMEM,
        )(ids, occupied)
        spread, slab = lax.optimization_barrier((spread, three_index))
        own = pl.pallas_call(
            hold_kernel,
            out_shape=jax.ShapeDtypeStruct(slab.shape, BF16),
            in_specs=[VMEM],
            out_specs=VMEM,
            compiler_params=pltpu.CompilerParams(vmem_limit_bytes=8 * 1024 * 1024),
        )(slab)
        own, slab = lax.optimization_barrier((own, slab))
        same_core = lax.all_to_all(spread, "orb", 0, 0, axis_index_groups=across, tiled=True)
        both = lax.all_gather(same_core, "orb", axis=0, axis_index_groups=pairs)
        pair = [
            lax.dynamic_slice(both, (c, place, rows * nocc // 128, 0), (1, 1, keep, tiles))
            for c, place in ((c, (chip + chips - jnp.where(c == 0, *FIRST_CHIP)) % chips) for c in (core, 1 - core))
        ]
        ids, theirs = (i.reshape(keep, tiles).astype(jnp.int32) for i in pair)
    with jax.named_scope("sibling_slab"):
        sibling = lax.ppermute(slab, "orb", [(i, i ^ 1) for i in range(n_orb)])

    depth = 2 * p_dev * nocc
    core = core.reshape(1).astype(jnp.int32)
    wire = (chips, wire_rows(rows, basis), 128)
    with jax.named_scope("order_coefficients"):
        coef = pl.pallas_call(
            functools.partial(order_kernel, FIRST_CHIP, basis),
            out_shape=jax.ShapeDtypeStruct((basis + width, nocc), BF16),
            in_specs=[VMEM],
            out_specs=VMEM,
            compiler_params=pltpu.CompilerParams(vmem_limit_bytes=8 * 1024 * 1024),
            cost_estimate=pl.CostEstimate(flops=ORDER_COST, bytes_accessed=0, transcendentals=0),
        )(both)
    with jax.named_scope("exchange"):
        sums = pl.pallas_call(
            functools.partial(exchange_kernel, FIRST_CHIP),
            out_shape=jax.ShapeDtypeStruct(wire, jnp.int16),
            in_specs=[SMEM, SMEM, SMEM, VMEM, VMEM, VMEM],
            out_specs=VMEM,
            scratch_shapes=[
                pltpu.VMEM((basis, depth), BF16),
                pltpu.VMEM((chips * rows, depth), BF16),
                pltpu.VMEM((chips, 8, 128), F32),
            ],
            compiler_params=pltpu.CompilerParams(vmem_limit_bytes=12 * 1024 * 1024),
        )(ids, theirs, core, coef, own, sibling)
    with jax.named_scope("sum_over_chips"):
        sums = lax.all_to_all(sums, "orb", 0, 0, axis_index_groups=across, tiled=True)
        sums = pl.pallas_call(
            functools.partial(group_sum_kernel, FIRST_AUX, rows, columns),
            out_shape=jax.ShapeDtypeStruct((n_aux, slot // 2, 128), jnp.int16),
            in_specs=[VMEM],
            out_specs=VMEM,
            compiler_params=pltpu.CompilerParams(vmem_limit_bytes=8 * 1024 * 1024),
        )(sums)
    with jax.named_scope("sum_over_aux"):
        sums = lax.all_to_all(sums, "aux", 0, 0, axis_index_groups=along, tiled=True)
        total_aux = p_dev * n_aux * n_orb
        return pl.pallas_call(
            functools.partial(final_sum_kernel, float(total_aux * nocc) ** -0.5),
            out_shape=jax.ShapeDtypeStruct((rows, columns), F32),
            in_specs=[VMEM],
            out_specs=VMEM,
            compiler_params=pltpu.CompilerParams(vmem_limit_bytes=4 * 1024 * 1024),
        )(sums)


def solution(mesh):
    return jax.shard_map(
        per_device,
        mesh=mesh,
        in_specs=(P(("aux", "orb"), None, None), P(("aux", "orb"), None, None), P("orb", None)),
        out_specs=P("orb", "aux"),
        check_vma=False,
    )
```
